32 devices in a mesh: shot: 2 (over x), dom: 16 (over z, y, core).
Axes of the slice: x: 2, y: 2, z: 4, core: 2. Of those that a mesh axis runs over, the one named last changes fastest.
Arguments:
- fwd_state: float32 [2, 9, 128, 16, 128], P('shot', None, 'dom'), may hold values from -6 to 6
- adj_state: float32 [2, 9, 128, 16, 128], P('shot', None, 'dom'), may hold values from -6 to 6
- stiff_normal: float32 [3, 128, 16, 128], P(None, 'dom'), may hold values from 0.18 to 0.3
- stiff_coupling: float32 [3, 128, 16, 128], P(None, 'dom'), may hold values from 0.03 to 0.08
- stiff_shear: float32 [3, 128, 16, 128], P(None, 'dom'), may hold values from 0.05 to 0.15
- buoyancy: float32 [128, 16, 128], P('dom'), may hold values from 0.25 to 0.5
- wavelet: float32 [2, 3], P('shot'), may hold values from -16 to 16
- residual: float32 [2, 3, 256], P('shot'), may hold values from -16 to 16
- source_cell: int32 [2], P('shot'), may hold values from 0 to 262143
- receiver_cell: int32 [2, 256], P('shot'), may hold values from 0 to 262143
Outputs:
- gradient: float32 [10, 128, 16, 128], P(None, 'dom', 'shot')
The draws below stay inside these ranges and needn't reach their ends.
All inputs are finite; a program needn't handle non-finite values.
Results may differ from the reference program's by a relative error of at most 0.00002.
Values sent between devices are 32-bit elements; how exact they have to be, the bound alone decides.
A program may use at most 64 MiB of HBM per device.

```python
import jax
import jax.numpy as jnp
from jax import lax

NREC = 256
ITERS = 3
NX = 128
NY = 16
NZ = 128
SHOTS = 2


def plant(entries, rng, low, high):
    place = [jax.random.randint(jax.random.fold_in(rng, axis), (), 0, length) for axis, length in enumerate(entries.shape)]
    widest = entries.shape.index(max(entries.shape))
    beside = place[:widest] + [(place[widest] + 1) % entries.shape[widest]] + place[widest + 1:]
    return entries.at[tuple(place)].set(low).at[tuple(beside)].set(high)


def block_scale(rng, shape, cuts, smallest, high):
    factor_of = 1.0
    for position, blocks in cuts:
        heights = jax.random.uniform(jax.random.fold_in(jax.random.fold_in(rng, 6), position), (blocks,), jnp.float32, smallest / len(cuts), high / len(cuts))
        factor_of = factor_of * jnp.repeat(jnp.exp(heights), shape[position] // blocks).reshape((-1,) + (1,) * (len(shape) - 1 - position))
    return factor_of


def bell_draw(own_key, extent, spread, bound, shards=(), kind=jnp.bfloat16):
    gain = block_scale(own_key, extent, shards, -0.22, 0.18) if shards else 1.0
    entries = jax.random.normal(own_key, extent, jnp.float32) * spread * gain
    return jnp.minimum(jnp.maximum(entries, -bound), bound).astype(kind)


def setup_inputs(seed: int = 0) -> dict:
    key_list = jax.random.split(jax.random.key(seed), 11)
    return {
        "fwd_state": bell_draw(key_list[0], (SHOTS, 9, NX, NY, NZ), 1.0, 6.0, ((0, 2), (2, 16)), jnp.float32),
        "adj_state": bell_draw(key_list[1], (SHOTS, 9, NX, NY, NZ), 1.0, 6.0, ((0, 2), (2, 16)), jnp.float32),
        "stiff_normal": jnp.clip(0.18 + 0.120000005 * jax.random.uniform(key_list[2], (3, NX, NY, NZ), jnp.float32) ** block_scale(key_list[2], (3, NX, NY, NZ), ((1, 16),), -0.2, 0.2), 0.18, 0.3),
        "stiff_coupling": jnp.clip(0.03 + 0.04999999888241291 * jax.random.uniform(key_list[3], (3, NX, NY, NZ), jnp.float32) ** block_scale(key_list[3], (3, NX, NY, NZ), ((1, 16),), -0.2, 0.2), 0.03, 0.08),
        "stiff_shear": jnp.clip(0.05 + 0.10000001 * jax.random.uniform(key_list[4], (3, NX, NY, NZ), jnp.float32) ** block_scale(key_list[4], (3, NX, NY, NZ), ((1, 16),), -0.2, 0.2), 0.05, 0.15),
        "buoyancy": jnp.clip(0.25 + 0.25 * jax.random.uniform(key_list[5], (NX, NY, NZ), jnp.float32) ** block_scale(key_list[5], (NX, NY, NZ), ((0, 16),), -0.2, 0.2), 0.25, 0.5),
        "wavelet": bell_draw(key_list[6], (SHOTS, ITERS), 4.0, 16.0, ((0, 2),), jnp.float32),
        "residual": bell_draw(key_list[7], (SHOTS, ITERS, NREC), 4.0, 16.0, ((0, 2),), jnp.float32),
        "source_cell": jax.random.randint(key_list[8], (SHOTS,), 0, NX * NY * NZ).astype(jnp.int32),
        "receiver_cell": plant(jax.random.randint(key_list[9], (SHOTS, NREC), 0, NX * NY * NZ), jax.random.fold_in(key_list[9], 1), 0, (NX * NY * NZ) - 1).astype(jnp.int32),
    }


stencil_taps = (1225.0 / 1024.0, -245.0 / 3072.0, 49.0 / 5120.0, -5.0 / 7168.0)


def derive(padded, axis_dim, margin, region_start, region_count, forward):
    result = jnp.zeros_like(lax.slice_in_dim(padded, 0, region_count, axis=axis_dim))
    for number in range(4):
        if forward:
            upper_at = margin + region_start + number + 1
            lower_at = margin + region_start - number
        else:
            upper_at = margin + region_start + number
            lower_at = margin + region_start - number - 1
        upper_part = lax.slice_in_dim(padded, upper_at, upper_at + region_count, axis=axis_dim)
        lower_part = lax.slice_in_dim(padded, lower_at, lower_at + region_count, axis=axis_dim)
        result = result + stencil_taps[number] * (upper_part - lower_part)
    return result


def along_axis(source, axis_dim, forward):
    widths = [(0, 0)] * source.ndim
    widths[axis_dim] = (4, 4)
    padded = jnp.pad(source, widths)
    return derive(padded, axis_dim, 4, 0, source.shape[axis_dim], forward)


def strain_set(velocity):
    strain_xx = along_axis(velocity[0], 1, False)
    strain_yy = along_axis(velocity[1], 2, False)
    strain_zz = along_axis(velocity[2], 3, False)
    strain_yz = along_axis(velocity[1], 3, True) + along_axis(velocity[2], 2, True)
    strain_xz = along_axis(velocity[0], 3, True) + along_axis(velocity[2], 1, True)
    strain_xy = along_axis(velocity[0], 2, True) + along_axis(velocity[1], 1, True)
    return [strain_xx, strain_yy, strain_zz, strain_yz, strain_xz, strain_xy]


def imaging(rebuilt, adjoint):
    return jnp.stack([
        rebuilt[0] * adjoint[0],
        rebuilt[1] * adjoint[1],
        rebuilt[2] * adjoint[2],
        rebuilt[0] * adjoint[1] + rebuilt[1] * adjoint[0],
        rebuilt[0] * adjoint[2] + rebuilt[2] * adjoint[0],
        rebuilt[1] * adjoint[2] + rebuilt[2] * adjoint[1],
        rebuilt[3] * adjoint[3],
        rebuilt[4] * adjoint[4],
        rebuilt[5] * adjoint[5],
        rebuilt[6] * adjoint[6] + rebuilt[7] * adjoint[7] + rebuilt[8] * adjoint[8],
    ])


def stress_update(stresses, strains, moduli, time_sign):
    return [
        stresses[0] + time_sign * (moduli[0] * strains[0] + moduli[3] * strains[1] + moduli[4] * strains[2]),
        stresses[1] + time_sign * (moduli[3] * strains[0] + moduli[1] * strains[1] + moduli[5] * strains[2]),
        stresses[2] + time_sign * (moduli[4] * strains[0] + moduli[5] * strains[1] + moduli[2] * strains[2]),
        stresses[3] + time_sign * (moduli[6] * strains[3]),
        stresses[4] + time_sign * (moduli[7] * strains[4]),
        stresses[5] + time_sign * (moduli[8] * strains[5]),
    ]


def reference(fwd_state, adj_state, stiff_normal, stiff_coupling, stiff_shear, buoyancy, wavelet, residual, source_cell, receiver_cell):
    time_sign = jnp.array([-1.0, 1.0], jnp.float32).reshape(2, 1, 1, 1)
    moduli = [stiff_normal[0], stiff_normal[1], stiff_normal[2], stiff_coupling[0], stiff_coupling[1], stiff_coupling[2], stiff_shear[0], stiff_shear[1], stiff_shear[2]]

    def one_shot(running, shot_data):
        rebuilt, adjoint, pulses, traces, source_at, receivers_at = shot_data
        velocity = [jnp.stack([rebuilt[component], adjoint[component]]) for component in range(3)]
        stresses = [jnp.stack([rebuilt[3 + component], adjoint[3 + component]]) for component in range(6)]
        for step_index in range(ITERS):
            strains = strain_set(velocity)
            factors = strains + velocity
            running = running + imaging([item[0] for item in factors], [item[1] for item in factors])
            stresses = stress_update(stresses, strains, moduli, time_sign)
            for number in range(3):
                flattened = stresses[number][0].reshape(-1).at[source_at].add(-pulses[step_index])
                stresses[number] = stresses[number].at[0].set(flattened.reshape(NX, NY, NZ))
            scaled = time_sign * buoyancy
            velocity = [
                velocity[0] + scaled * (along_axis(stresses[0], 1, True) + along_axis(stresses[5], 2, False) + along_axis(stresses[4], 3, False)),
                velocity[1] + scaled * (along_axis(stresses[5], 1, False) + along_axis(stresses[1], 2, True) + along_axis(stresses[3], 3, False)),
                velocity[2] + scaled * (along_axis(stresses[4], 1, False) + along_axis(stresses[3], 2, False) + along_axis(stresses[2], 3, True)),
            ]
            flattened = velocity[2][1].reshape(-1).at[receivers_at].add(traces[step_index])
            velocity[2] = velocity[2].at[1].set(flattened.reshape(NX, NY, NZ))
        return running, None

    initial = jnp.zeros((10, NX, NY, NZ), jnp.float32)
    running, unused = lax.scan(one_shot, initial, (fwd_state, adj_state, wavelet, residual, source_cell, receiver_cell))
    return running / ITERS
```

```python
import functools

import jax
import jax.numpy as jnp
from jax import lax
from jax.experimental import pallas as pl
from jax.experimental.pallas import tpu as pltpu
from jax.sharding import PartitionSpec as P

ITERS = 3
TAPS = (1225.0 / 1024.0, -245.0 / 3072.0, 49.0 / 5120.0, -5.0 / 7168.0)
MESH = pl.DeviceIdType.MESH
F32 = jnp.float32
BF16 = jnp.bfloat16

VEL_UP = ((slice(0, 1), 8, 0, 4), (slice(1, 3), 9, 1, 3))
VEL_DOWN = ((slice(0, 1), 4, 12, 3), (slice(1, 3), 4, 12, 4))
STR_UP = ((slice(0, 1), 9, 1, 3), (slice(1, 3), 8, 0, 4))
STR_DOWN = ((slice(0, 1), 4, 12, 4), (slice(1, 3), 4, 12, 3))


def split2(f):
    hi = f.astype(BF16)
    return hi, (f - hi.astype(F32)).astype(BF16)


def band(offset, forward):
    out = jnp.zeros(offset.shape, F32)
    for m in range(1, 5):
        plus, minus = (m, 1 - m) if forward else (m - 1, -m)
        out = jnp.where(offset == plus, F32(TAPS[m - 1]), out)
        out = jnp.where(offset == minus, F32(-TAPS[m - 1]), out)
    return out


def kernel(
    shots, doms, fwd, adj, cn, cc, cs, buoy, wav, res, src, rcv, out,
    V, S, T, C, B, E, Q, RI, GL, GX, RL, RX, MZ, MY,
    load_sem, ssem, rsem, gs_sem, gr_sem,
):
    nx, ny, nz = 8, V.shape[3], V.shape[4]
    rows = nx * ny
    yp = ny // shots
    dom = lax.axis_index("dom")
    shot = lax.axis_index("shot")
    has_lo = dom > 0
    has_hi = dom < doms - 1
    above = lax.rem(dom + 1, doms)
    below = lax.rem(dom + doms - 1, doms)

    loads = []

    def load(a, b):
        c = pltpu.make_async_copy(a, b, load_sem.at[len(loads)])
        c.start()
        loads.append(c)

    states = (fwd, adj)
    for w in range(2):
        load(states[w].at[0, 0:3], V.at[w, :, pl.ds(4, nx)])
    for w in range(2):
        load(states[w].at[0, 3], S.at[w, 0, pl.ds(4, nx)])
        load(states[w].at[0, 8], S.at[w, 1, pl.ds(4, nx)])
        load(states[w].at[0, 7], S.at[w, 2, pl.ds(4, nx)])
        load(states[w].at[0, 4:7], T.at[w])
    load(cn, C.at[0:3])
    load(cc, C.at[3:6])
    load(cs, C.at[6:9])
    load(buoy, B)

    barrier = pltpu.get_barrier_semaphore()

    @pl.when(has_lo)
    def _():
        pl.semaphore_signal(barrier, inc=1, device_id={"dom": below}, device_id_type=MESH)

    @pl.when(has_hi)
    def _():
        pl.semaphore_signal(barrier, inc=1, device_id={"dom": above}, device_id_type=MESH)

    for o in range(1, shots):
        pl.semaphore_signal(
            barrier, inc=1, device_id={"shot": lax.rem(shot + o, shots)}, device_id_type=MESH
        )

    @pl.when(jnp.logical_not(has_lo))
    def _():
        V[:, :, 0:4] = jnp.zeros((2, 3, 4, ny, nz), F32)
        S[:, :, 0:4] = jnp.zeros((2, 3, 4, ny, nz), F32)

    @pl.when(jnp.logical_not(has_hi))
    def _():
        V[:, :, 12:16] = jnp.zeros((2, 3, 4, ny, nz), F32)
        S[:, :, 12:16] = jnp.zeros((2, 3, 4, ny, nz), F32)

    pl.semaphore_wait(
        barrier, has_lo.astype(jnp.int32) + has_hi.astype(jnp.int32) + (shots - 1)
    )

    def message(stage, w, side):
        buf = S if stage % 2 else V
        plan = ((VEL_UP, VEL_DOWN), (STR_UP, STR_DOWN))[stage % 2][side]
        copies = []
        for piece, (comp, at, to, count) in enumerate(plan):
            if stage == 0:
                source = states[w].at[0, comp, pl.ds(at - 4, count)]
            else:
                source = buf.at[w, comp, pl.ds(at, count)]
            copies.append(
                pltpu.make_async_remote_copy(
                    src_ref=source,
                    dst_ref=buf.at[w, comp, pl.ds(to, count)],
                    send_sem=ssem.at[stage, w, side, piece],
                    recv_sem=rsem.at[stage, w, side, piece],
                    device_id={"dom": below if side else above},
                    device_id_type=MESH,
                )
            )
        return copies

    def send(stage, w):
        @pl.when(has_hi)
        def _():
            for c in message(stage, w, 0):
                c.start()

        @pl.when(has_lo)
        def _():
            for c in message(stage, w, 1):
                c.start()

    def wait_send(stage, w):
        @pl.when(has_hi)
        def _():
            for c in message(stage, w, 0):
                c.wait_send()

        @pl.when(has_lo)
        def _():
            for c in message(stage, w, 1):
                c.wait_send()

    def wait_recv(stage, w):
        @pl.when(has_lo)
        def _():
            for c in message(stage, w, 0):
                c.wait_recv()

        @pl.when(has_hi)
        def _():
            for c in message(stage, w, 1):
                c.wait_recv()

    for w in range(2):
        send(0, w)

    r = lax.broadcasted_iota(jnp.int32, (nz, nz), 0)
    c = lax.broadcasted_iota(jnp.int32, (nz, nz), 1)
    for f in range(2):
        hi, mid = split2(band(r - c, f == 1))
        half = jnp.concatenate([hi, mid], axis=1)
        MZ[f] = jnp.concatenate([half, half], axis=0)
    r = lax.broadcasted_iota(jnp.int32, (rows, rows), 0)
    c = lax.broadcasted_iota(jnp.int32, (rows, rows), 1)
    for f in range(2):
        coef = jnp.where(r // ny == c // ny, band(c - r, f == 1), F32(0.0))
        hi, mid = split2(coef)
        half = jnp.concatenate([hi, mid], axis=0)
        MY[f] = jnp.concatenate([half, half], axis=1)

    cell = rcv[...]
    local = cell - dom * (rows * nz)
    cell_row = lax.shift_right_arithmetic(local, 7)
    cell_z = jnp.bitwise_and(local, 127)
    nrec = cell.shape[1]
    at_row = lax.broadcasted_iota(jnp.int32, (rows, nrec), 0) == cell_row
    at_z = (lax.broadcasted_iota(jnp.int32, (nz, nrec), 0) == cell_z).astype(F32).astype(BF16)
    for k in range(ITERS - 1):
        a = jnp.where(at_row, res[0, k : k + 1, :], F32(0.0))
        hi, mid = split2(a)
        low = (a - hi.astype(F32) - mid.astype(F32)).astype(BF16)
        total = None
        for part in (low, mid, hi):
            d = lax.dot_general(
                part, at_z, (((1,), (1,)), ((), ())), preferred_element_type=F32
            )
            total = d if total is None else total + d
        RI[k] = total.reshape(nx, ny, nz)

    def zd(fields, forward):
        f = fields.reshape(-1, nz)
        hi, mid = split2(f)
        d = jnp.dot(
            jnp.concatenate([hi, mid], axis=1), MZ[int(forward)], preferred_element_type=F32
        )
        return (d[:, :nz] + d[:, nz:]).reshape(fields.shape)

    def yd(field, forward):
        hi, mid = split2(field.reshape(rows, nz))
        d = jnp.dot(
            MY[int(forward)], jnp.concatenate([hi, mid], axis=0), preferred_element_type=F32
        )
        return (d[:rows] + d[rows:]).reshape(nx, ny, nz)

    def xd(buf, w, comp, forward):
        total = None
        for m in range(1, 5):
            p, q = (m, 1 - m) if forward else (m - 1, -m)
            t = F32(TAPS[m - 1]) * (
                buf[w, comp, 4 + p : 4 + p + nx] - buf[w, comp, 4 + q : 4 + q + nx]
            )
            total = t if total is None else total + t
        return total

    def own(buf, w, comp):
        return buf[w, comp, 4 : 4 + nx]

    def local_strains(w):
        E[w, 1] = yd(own(V, w, 1), False)
        E[w, 2] = zd(own(V, w, 2), False)
        E[w, 3] = zd(own(V, w, 1), True) + yd(own(V, w, 2), True)
        E[w, 4] = zd(own(V, w, 0), True)
        E[w, 5] = yd(own(V, w, 0), True)

    def x_strains(w):
        E[w, 0] = xd(V, w, 0, False)
        E[w, 4] = E[w, 4] + xd(V, w, 2, True)
        E[w, 5] = E[w, 5] + xd(V, w, 1, True)

    def put(g, i, value, first):
        for p in range(shots):
            part = value[:, p * yp : (p + 1) * yp, :]
            g[p, i] = part if first else g[p, i] + part

    def image_local(first):
        put(GL, 0, E[0, 1] * E[1, 1], first)
        put(GL, 1, E[0, 2] * E[1, 2], first)
        put(GL, 2, E[0, 1] * E[1, 2] + E[0, 2] * E[1, 1], first)
        put(GL, 3, E[0, 3] * E[1, 3], first)
        put(
            GL, 4,
            own(V, 0, 0) * own(V, 1, 0) + own(V, 0, 1) * own(V, 1, 1)
            + own(V, 0, 2) * own(V, 1, 2),
            first,
        )

    def image_x(first):
        put(GX, 0, E[0, 0] * E[1, 0], first)
        put(GX, 1, E[0, 0] * E[1, 1] + E[0, 1] * E[1, 0], first)
        put(GX, 2, E[0, 0] * E[1, 2] + E[0, 2] * E[1, 0], first)
        put(GX, 3, E[0, 4] * E[1, 4], first)
        put(GX, 4, E[0, 5] * E[1, 5], first)

    def source_field(k):
        at = (
            lax.broadcasted_iota(jnp.int32, (nx, ny, nz), 0) * (ny * nz)
            + lax.broadcasted_iota(jnp.int32, (nx, ny, nz), 1) * nz
            + lax.broadcasted_iota(jnp.int32, (nx, ny, nz), 2)
        )
        return jnp.where(at == src[0] - dom * (rows * nz), wav[0, k], F32(0.0))

    def signed(w, base, change):
        return base + change if w else base - change

    def sums(g, landing, group):
        copies = []
        for o in range(1, shots):
            to = lax.rem(shot + o, shots)
            copies.append(
                pltpu.make_async_remote_copy(
                    src_ref=g.at[to],
                    dst_ref=landing.at[o - 1],
                    send_sem=gs_sem.at[group, o - 1],
                    recv_sem=gr_sem.at[group, o - 1],
                    device_id={"shot": to},
                    device_id_type=MESH,
                )
            )
        return copies

    loads[0].wait()
    loads[1].wait()
    for k in range(ITERS):
        for w in range(2):
            local_strains(w)
        if k == ITERS - 1:
            break
        if k == 0:
            for copy in loads[2:]:
                copy.wait()
        for w in range(2):
            wait_recv(2 * k, w)
            x_strains(w)
            if k:
                wait_send(2 * k - 1, w)
            exx, eyy, ezz = E[w, 0], E[w, 1], E[w, 2]
            sxx = signed(w, own(S, w, 0), C[0] * exx + C[3] * eyy + C[4] * ezz)
            if w == 0:
                sxx = sxx - source_field(k)
            S[w, 0, 4 : 4 + nx] = sxx
            S[w, 1, 4 : 4 + nx] = signed(w, own(S, w, 1), C[8] * E[w, 5])
            S[w, 2, 4 : 4 + nx] = signed(w, own(S, w, 2), C[7] * E[w, 4])
            send(2 * k + 1, w)
        for w in range(2):
            exx, eyy, ezz = E[w, 0], E[w, 1], E[w, 2]
            syy = signed(w, T[w, 0], C[3] * exx + C[1] * eyy + C[5] * ezz)
            szz = signed(w, T[w, 1], C[4] * exx + C[5] * eyy + C[2] * ezz)
            if w == 0:
                pulse = source_field(k)
                syy = syy - pulse
                szz = szz - pulse
            syz = signed(w, T[w, 2], C[6] * E[w, 3])
            T[w, 0] = syy
            T[w, 1] = szz
            T[w, 2] = syz
            Q[w, 0] = yd(own(S, w, 1), False) + zd(own(S, w, 2), False)
            Q[w, 1] = yd(syy, True) + zd(syz, False)
            Q[w, 2] = yd(syz, False) + zd(szz, True)
        image_local(k == 0)
        image_x(k == 0)
        for w in range(2):
            wait_recv(2 * k + 1, w)
            vx = signed(w, own(V, w, 0), B[...] * (xd(S, w, 0, True) + Q[w, 0]))
            vy = signed(w, own(V, w, 1), B[...] * (xd(S, w, 1, False) + Q[w, 1]))
            vz = signed(w, own(V, w, 2), B[...] * (xd(S, w, 2, False) + Q[w, 2]))
            if w:
                vz = vz + RI[k]
            if k:
                wait_send(2 * k, w)
            V[w, 0, 4 : 4 + nx] = vx
            V[w, 1, 4 : 4 + nx] = vy
            V[w, 2, 4 : 4 + nx] = vz
            send(2 * k + 2, w)

    image_local(False)
    for copy in sums(GL, RL, 0):
        copy.start()
    for w in range(2):
        wait_recv(2 * ITERS - 2, w)
        x_strains(w)
    image_x(False)
    for copy in sums(GX, RX, 1):
        copy.start()
    scale = F32(1.0 / ITERS)
    slots = ((1, 2, 5, 6, 9), (0, 3, 4, 7, 8))
    for group, (g, landing) in enumerate(((GL, RL), (GX, RX))):
        for copy in sums(g, landing, group):
            copy.wait_recv()
        for i, slot in enumerate(slots[group]):
            total = g[shot, i]
            for o in range(shots - 1):
                total = total + landing[o, i]
            out[slot] = total * scale
    for w in range(2):
        wait_send(0, w)
        wait_send(2 * ITERS - 3, w)
        wait_send(2 * ITERS - 2, w)
    for group, (g, landing) in enumerate(((GL, RL), (GX, RX))):
        for copy in sums(g, landing, group):
            copy.wait_send()


def body(shots, doms, fwd, adj, cn, cc, cs, buoy, wav, res, src, rcv):
    nx, ny, nz = buoy.shape
    field = (nx, ny, nz)
    yp = ny // shots
    wide = nx + 8
    stages = 2 * ITERS - 1
    hbm = pl.BlockSpec(memory_space=pl.ANY)
    vmem = pl.BlockSpec(memory_space=pltpu.VMEM)
    smem = pl.BlockSpec(memory_space=pltpu.SMEM)
    return pl.pallas_call(
        functools.partial(kernel, shots, doms),
        out_shape=jax.ShapeDtypeStruct((10, nx, yp, nz), F32),
        in_specs=[hbm] * 6 + [smem, vmem, smem, vmem],
        out_specs=vmem,
        scratch_shapes=[
            pltpu.VMEM((2, 3, wide, ny, nz), F32),
            pltpu.VMEM((2, 3, wide, ny, nz), F32),
            pltpu.VMEM((2, 3) + field, F32),
            pltpu.VMEM((9,) + field, F32),
            pltpu.VMEM(field, F32),
            pltpu.VMEM((2, 6) + field, F32),
            pltpu.VMEM((2, 3) + field, F32),
            pltpu.VMEM((ITERS - 1,) + field, F32),
            pltpu.VMEM((shots, 5, nx, yp, nz), F32),
            pltpu.VMEM((shots, 5, nx, yp, nz), F32),
            pltpu.VMEM((shots - 1, 5, nx, yp, nz), F32),
            pltpu.VMEM((shots - 1, 5, nx, yp, nz), F32),
            pltpu.VMEM((2, 2 * nz, 2 * nz), BF16),
            pltpu.VMEM((2, 2 * nx * ny, 2 * nx * ny), BF16),
            pltpu.SemaphoreType.DMA((14,)),
            pltpu.SemaphoreType.DMA((stages, 2, 2, 2)),
            pltpu.SemaphoreType.DMA((stages, 2, 2, 2)),
            pltpu.SemaphoreType.DMA((2, shots - 1)),
            pltpu.SemaphoreType.DMA((2, shots - 1)),
        ],
        compiler_params=pltpu.CompilerParams(
            collective_id=0, has_side_effects=True, vmem_limit_bytes=48 * 1024 * 1024
        ),
    )(fwd, adj, cn, cc, cs, buoy, wav, res, src, rcv)


def solution(mesh):
    placed = (
        P("shot", None, "dom", None, None),
        P("shot", None, "dom", None, None),
        P(None, "dom", None, None),
        P(None, "dom", None, None),
        P(None, "dom", None, None),
        P("dom", None, None),
        P("shot", None),
        P("shot", None, None),
        P("shot"),
        P("shot", None),
    )
    return jax.shard_map(
        functools.partial(body, mesh.shape["shot"], mesh.shape["dom"]),
        mesh=mesh,
        in_specs=placed,
        out_specs=P(None, "dom", "shot", None),
        check_vma=False,
    )
```

```python
import functools

import jax
import jax.numpy as jnp
from jax import lax
from jax.experimental import pallas as pl
from jax.experimental.pallas import tpu as pltpu
from jax.sharding import PartitionSpec as P

ITERS = 3
TAPS = (1225.0 / 1024.0, -245.0 / 3072.0, 49.0 / 5120.0, -5.0 / 7168.0)
MESH = pl.DeviceIdType.MESH
F32 = jnp.float32
BF16 = jnp.bfloat16

VEL_UP = ((slice(0, 1), 4), (slice(1, 3), 3))
VEL_DOWN = ((slice(0, 1), 3), (slice(1, 3), 4))
STR_UP = ((slice(0, 1), 3), (slice(1, 3), 4))
STR_DOWN = ((slice(0, 1), 4), (slice(1, 3), 3))


def split2(f):
    hi = f.astype(BF16)
    return hi, (f - hi.astype(F32)).astype(BF16)


def band(offset, forward):
    out = jnp.zeros(offset.shape, F32)
    for m in range(1, 5):
        plus, minus = (m, 1 - m) if forward else (m - 1, -m)
        out = jnp.where(offset == plus, F32(TAPS[m - 1]), out)
        out = jnp.where(offset == minus, F32(-TAPS[m - 1]), out)
    return out


def kernel(
    shots, doms, fwd, adj, cn, cc, cs, buoy, wav, res, src, rcv, out,
    V, S, T, C, B, E, Q, RI, GL, GX, RL, RX, MZ, MY,
    load_sem, ssem, rsem, gs_sem, gr_sem,
):
    nx, ny, nz = B.shape
    rows = nx * ny
    yp = ny // shots
    dom = lax.axis_index("dom")
    shot = lax.axis_index("shot")
    has_lo = dom > 0
    has_hi = dom < doms - 1
    above = lax.rem(dom + 1, doms)
    below = lax.rem(dom + doms - 1, doms)

    loads = []

    def load(a, b):
        c = pltpu.make_async_copy(a, b, load_sem.at[len(loads)])
        c.start()
        loads.append(c)

    states = (fwd, adj)
    for w in range(2):
        load(states[w].at[0, 0:3], V.at[w, :, pl.ds(4, nx)])
    for w in range(2):
        load(states[w].at[0, 3], S.at[w, 0, pl.ds(4, nx)])
        load(states[w].at[0, 8], S.at[w, 1, pl.ds(4, nx)])
        load(states[w].at[0, 7], S.at[w, 2, pl.ds(4, nx)])
        load(states[w].at[0, 4:7], T.at[w])
    load(cn, C.at[0:3])
    load(cc, C.at[3:6])
    load(cs, C.at[6:9])
    load(buoy, B)

    barrier = pltpu.get_barrier_semaphore()

    @pl.when(has_lo)
    def _():
        pl.semaphore_signal(barrier, inc=1, device_id={"dom": below}, device_id_type=MESH)

    @pl.when(has_hi)
    def _():
        pl.semaphore_signal(barrier, inc=1, device_id={"dom": above}, device_id_type=MESH)

    for o in range(1, shots):
        pl.semaphore_signal(
            barrier, inc=1, device_id={"shot": lax.rem(shot + o, shots)}, device_id_type=MESH
        )

    @pl.when(jnp.logical_not(has_lo))
    def _():
        V[:, :, 0:4] = jnp.zeros((2, 3, 4, ny, nz), F32)
        S[:, :, 0:4] = jnp.zeros((2, 3, 4, ny, nz), F32)

    @pl.when(jnp.logical_not(has_hi))
    def _():
        V[:, :, 4 + nx : 8 + nx] = jnp.zeros((2, 3, 4, ny, nz), F32)
        S[:, :, 4 + nx : 8 + nx] = jnp.zeros((2, 3, 4, ny, nz), F32)

    pl.semaphore_wait(
        barrier, has_lo.astype(jnp.int32) + has_hi.astype(jnp.int32) + (shots - 1)
    )

    def message(stage, w, side):
        buf = S if stage % 2 else V
        plan = ((VEL_UP, VEL_DOWN), (STR_UP, STR_DOWN))[stage % 2][side]
        copies = []
        for piece, (comp, count) in enumerate(plan):
            at, to = (4, 4 + nx) if side else (4 + nx - count, 4 - count)
            if stage == 0:
                source = states[w].at[0, comp, pl.ds(at - 4, count)]
            else:
                source = buf.at[w, comp, pl.ds(at, count)]
            copies.append(
                pltpu.make_async_remote_copy(
                    src_ref=source,
                    dst_ref=buf.at[w, comp, pl.ds(to, count)],
                    send_sem=ssem.at[stage, w, side, piece],
                    recv_sem=rsem.at[stage, w, side, piece],
                    device_id={"dom": below if side else above},
                    device_id_type=MESH,
                )
            )
        return copies

    def send(stage, w):
        @pl.when(has_hi)
        def _():
            for c in message(stage, w, 0):
                c.start()

        @pl.when(has_lo)
        def _():
            for c in message(stage, w, 1):
                c.start()

    def wait_send(stage, w):
        @pl.when(has_hi)
        def _():
            for c in message(stage, w, 0):
                c.wait_send()

        @pl.when(has_lo)
        def _():
            for c in message(stage, w, 1):
                c.wait_send()

    def wait_recv(stage, w):
        @pl.when(has_lo)
        def _():
            for c in message(stage, w, 0):
                c.wait_recv()

        @pl.when(has_hi)
        def _():
            for c in message(stage, w, 1):
                c.wait_recv()

    for w in range(2):
        send(0, w)

    r = lax.broadcasted_iota(jnp.int32, (nz, nz), 0)
    c = lax.broadcasted_iota(jnp.int32, (nz, nz), 1)
    for f in range(2):
        hi, mid = split2(band(r - c, f == 1))
        half = jnp.concatenate([hi, mid], axis=1)
        MZ[f] = jnp.concatenate([half, half], axis=0)
    r = lax.broadcasted_iota(jnp.int32, (rows, rows), 0)
    c = lax.broadcasted_iota(jnp.int32, (rows, rows), 1)
    for f in range(2):
        coef = jnp.where(r // ny == c // ny, band(c - r, f == 1), F32(0.0))
        hi, mid = split2(coef)
        half = jnp.concatenate([hi, mid], axis=0)
        MY[f] = jnp.concatenate([half, half], axis=1)

    cell = rcv[...]
    local = cell - dom * (rows * nz)
    cell_row = local // nz
    cell_z = local - nz * cell_row
    nrec = cell.shape[1]
    at_row = lax.broadcasted_iota(jnp.int32, (rows, nrec), 0) == cell_row
    at_z = (lax.broadcasted_iota(jnp.int32, (nz, nrec), 0) == cell_z).astype(F32).astype(BF16)
    for k in range(ITERS - 1):
        a = jnp.where(at_row, res[k], F32(0.0))
        hi, mid = split2(a)
        low = (a - hi.astype(F32) - mid.astype(F32)).astype(BF16)
        total = None
        for part in (low, mid, hi):
            d = lax.dot_general(
                part, at_z, (((1,), (1,)), ((), ())), preferred_element_type=F32
            )
            total = d if total is None else total + d
        RI[k] = total.reshape(nx, ny, nz)

    def zd(fields, forward):
        f = fields.reshape(-1, nz)
        hi, mid = split2(f)
        d = jnp.dot(
            jnp.concatenate([hi, mid], axis=1), MZ[int(forward)], preferred_element_type=F32
        )
        return (d[:, :nz] + d[:, nz:]).reshape(fields.shape)

    def yd(field, forward):
        hi, mid = split2(field.reshape(rows, nz))
        d = jnp.dot(
            MY[int(forward)], jnp.concatenate([hi, mid], axis=0), preferred_element_type=F32
        )
        return (d[:rows] + d[rows:]).reshape(nx, ny, nz)

    def xd(buf, w, comp, forward):
        total = None
        for m in range(1, 5):
            p, q = (m, 1 - m) if forward else (m - 1, -m)
            t = F32(TAPS[m - 1]) * (
                buf[w, comp, 4 + p : 4 + p + nx] - buf[w, comp, 4 + q : 4 + q + nx]
            )
            total = t if total is None else total + t
        return total

    def own(buf, w, comp):
        return buf[w, comp, 4 : 4 + nx]

    def local_strains(w):
        E[w, 1] = yd(own(V, w, 1), False)
        E[w, 2] = zd(own(V, w, 2), False)
        E[w, 3] = zd(own(V, w, 1), True) + yd(own(V, w, 2), True)
        E[w, 4] = zd(own(V, w, 0), True)
        E[w, 5] = yd(own(V, w, 0), True)

    def x_strains(w):
        E[w, 0] = xd(V, w, 0, False)
        E[w, 4] = E[w, 4] + xd(V, w, 2, True)
        E[w, 5] = E[w, 5] + xd(V, w, 1, True)

    def put(g, i, value, first):
        for p in range(shots):
            part = value[:, p * yp : (p + 1) * yp, :]
            g[p, i] = part if first else g[p, i] + part

    def image_local(first):
        put(GL, 0, E[0, 1] * E[1, 1], first)
        put(GL, 1, E[0, 2] * E[1, 2], first)
        put(GL, 2, E[0, 1] * E[1, 2] + E[0, 2] * E[1, 1], first)
        put(GL, 3, E[0, 3] * E[1, 3], first)
        put(
            GL, 4,
            own(V, 0, 0) * own(V, 1, 0) + own(V, 0, 1) * own(V, 1, 1)
            + own(V, 0, 2) * own(V, 1, 2),
            first,
        )

    def image_x(first):
        put(GX, 0, E[0, 0] * E[1, 0], first)
        put(GX, 1, E[0, 0] * E[1, 1] + E[0, 1] * E[1, 0], first)
        put(GX, 2, E[0, 0] * E[1, 2] + E[0, 2] * E[1, 0], first)
        put(GX, 3, E[0, 4] * E[1, 4], first)
        put(GX, 4, E[0, 5] * E[1, 5], first)

    def source_field(k):
        at = (
            lax.broadcasted_iota(jnp.int32, (nx, ny, nz), 0) * (ny * nz)
            + lax.broadcasted_iota(jnp.int32, (nx, ny, nz), 1) * nz
            + lax.broadcasted_iota(jnp.int32, (nx, ny, nz), 2)
        )
        return jnp.where(at == src[0] - dom * (rows * nz), wav[0, k], F32(0.0))

    def signed(w, base, change):
        return base + change if w else base - change

    def sums(g, landing, group):
        copies = []
        for o in range(1, shots):
            to = lax.rem(shot + o, shots)
            copies.append(
                pltpu.make_async_remote_copy(
                    src_ref=g.at[to],
                    dst_ref=landing.at[o - 1],
                    send_sem=gs_sem.at[group, o - 1],
                    recv_sem=gr_sem.at[group, o - 1],
                    device_id={"shot": to},
                    device_id_type=MESH,
                )
            )
        return copies

    loads[0].wait()
    loads[1].wait()
    for k in range(ITERS):
        for w in range(2):
            local_strains(w)
        if k == ITERS - 1:
            break
        if k == 0:
            for copy in loads[2:]:
                copy.wait()
        for w in range(2):
            wait_recv(2 * k, w)
            x_strains(w)
            if k:
                wait_send(2 * k - 1, w)
            exx, eyy, ezz = E[w, 0], E[w, 1], E[w, 2]
            sxx = signed(w, own(S, w, 0), C[0] * exx + C[3] * eyy + C[4] * ezz)
            if w == 0:
                sxx = sxx - source_field(k)
            S[w, 0, 4 : 4 + nx] = sxx
            S[w, 1, 4 : 4 + nx] = signed(w, own(S, w, 1), C[8] * E[w, 5])
            S[w, 2, 4 : 4 + nx] = signed(w, own(S, w, 2), C[7] * E[w, 4])
            send(2 * k + 1, w)
        for w in range(2):
            exx, eyy, ezz = E[w, 0], E[w, 1], E[w, 2]
            syy = signed(w, T[w, 0], C[3] * exx + C[1] * eyy + C[5] * ezz)
            szz = signed(w, T[w, 1], C[4] * exx + C[5] * eyy + C[2] * ezz)
            if w == 0:
                pulse = source_field(k)
                syy = syy - pulse
                szz = szz - pulse
            syz = signed(w, T[w, 2], C[6] * E[w, 3])
            T[w, 0] = syy
            T[w, 1] = szz
            T[w, 2] = syz
            Q[w, 0] = yd(own(S, w, 1), False) + zd(own(S, w, 2), False)
            Q[w, 1] = yd(syy, True) + zd(syz, False)
            Q[w, 2] = yd(syz, False) + zd(szz, True)
        image_local(k == 0)
        image_x(k == 0)
        for w in range(2):
            wait_recv(2 * k + 1, w)
            vx = signed(w, own(V, w, 0), B[...] * (xd(S, w, 0, True) + Q[w, 0]))
            vy = signed(w, own(V, w, 1), B[...] * (xd(S, w, 1, False) + Q[w, 1]))
            vz = signed(w, own(V, w, 2), B[...] * (xd(S, w, 2, False) + Q[w, 2]))
            if w:
                vz = vz + RI[k]
            if k:
                wait_send(2 * k, w)
            V[w, 0, 4 : 4 + nx] = vx
            V[w, 1, 4 : 4 + nx] = vy
            V[w, 2, 4 : 4 + nx] = vz
            send(2 * k + 2, w)

    image_local(False)
    for copy in sums(GL, RL, 0):
        copy.start()
    for w in range(2):
        wait_recv(2 * ITERS - 2, w)
        x_strains(w)
    image_x(False)
    for copy in sums(GX, RX, 1):
        copy.start()
    scale = F32(1.0 / ITERS)
    slots = ((1, 2, 5, 6, 9), (0, 3, 4, 7, 8))
    for group, (g, landing) in enumerate(((GL, RL), (GX, RX))):
        for copy in sums(g, landing, group):
            copy.wait_recv()
        for i, slot in enumerate(slots[group]):
            total = g[shot, i]
            for o in range(shots - 1):
                total = total + landing[o, i]
            out[slot] = total * scale
    for w in range(2):
        wait_send(0, w)
        wait_send(2 * ITERS - 3, w)
        wait_send(2 * ITERS - 2, w)
    for group, (g, landing) in enumerate(((GL, RL), (GX, RX))):
        for copy in sums(g, landing, group):
            copy.wait_send()


def body(shots, doms, fwd, adj, cn, cc, cs, buoy, wav, res, src, rcv):
    nx, ny, nz = buoy.shape
    field = (nx, ny, nz)
    yp = ny // shots
    wide = nx + 8
    stages = 2 * ITERS - 1
    hbm = pl.BlockSpec(memory_space=pltpu.HBM)
    vmem = pl.BlockSpec(memory_space=pltpu.VMEM)
    smem = pl.BlockSpec(memory_space=pltpu.SMEM)
    return pl.pallas_call(
        functools.partial(kernel, shots, doms),
        out_shape=jax.ShapeDtypeStruct((10, nx, yp, nz), F32),
        in_specs=[hbm] * 6 + [smem, vmem, smem, vmem],
        out_specs=vmem,
        scratch_shapes=[
            pltpu.VMEM((2, 3, wide, ny, nz), F32),
            pltpu.VMEM((2, 3, wide, ny, nz), F32),
            pltpu.VMEM((2, 3) + field, F32),
            pltpu.VMEM((9,) + field, F32),
            pltpu.VMEM(field, F32),
            pltpu.VMEM((2, 6) + field, F32),
            pltpu.VMEM((2, 3) + field, F32),
            pltpu.VMEM((ITERS - 1,) + field, F32),
            pltpu.VMEM((shots, 5, nx, yp, nz), F32),
            pltpu.VMEM((shots, 5, nx, yp, nz), F32),
            pltpu.VMEM((shots - 1, 5, nx, yp, nz), F32),
            pltpu.VMEM((shots - 1, 5, nx, yp, nz), F32),
            pltpu.VMEM((2, 2 * nz, 2 * nz), BF16),
            pltpu.VMEM((2, 2 * nx * ny, 2 * nx * ny), BF16),
            pltpu.SemaphoreType.DMA((14,)),
            pltpu.SemaphoreType.DMA((stages, 2, 2, 2)),
            pltpu.SemaphoreType.DMA((stages, 2, 2, 2)),
            pltpu.SemaphoreType.DMA((2, shots - 1)),
            pltpu.SemaphoreType.DMA((2, shots - 1)),
        ],
        compiler_params=pltpu.CompilerParams(
            collective_id=0, has_side_effects=True, vmem_limit_bytes=63 * 1024 * 1024
        ),
    )(fwd, adj, cn, cc, cs, buoy, wav, jnp.transpose(res, (1, 0, 2)), src, rcv)


def solution(mesh):
    placed = (
        P("shot", None, "dom", None, None),
        P("shot", None, "dom", None, None),
        P(None, "dom", None, None),
        P(None, "dom", None, None),
        P(None, "dom", None, None),
        P("dom", None, None),
        P("shot", None),
        P("shot", None, None),
        P("shot"),
        P("shot", None),
    )
    return jax.shard_map(
        functools.partial(body, mesh.shape["shot"], mesh.shape["dom"]),
        mesh=mesh,
        in_specs=placed,
        out_specs=P(None, "dom", "shot", None),
        check_vma=False,
    )
```

```python
import functools

import jax
import jax.numpy as jnp
from jax import lax
from jax.experimental import pallas as pl
from jax.experimental.pallas import tpu as pltpu
from jax.sharding import PartitionSpec as P

ITERS = 3
TAPS = (1225.0 / 1024.0, -245.0 / 3072.0, 49.0 / 5120.0, -5.0 / 7168.0)
MESH = pl.DeviceIdType.MESH
F32 = jnp.float32
BF16 = jnp.bfloat16

VEL_LAYERS = ((4, 3, 3), (3, 4, 4))
STR_LAYERS = ((3, 4, 4), (4, 3, 3))


def split2(f):
    hi = f.astype(BF16)
    return hi, (f - hi.astype(F32)).astype(BF16)


def band(offset, forward):
    out = jnp.zeros(offset.shape, F32)
    for m in range(1, 5):
        plus, minus = (m, 1 - m) if forward else (m - 1, -m)
        out = jnp.where(offset == plus, F32(TAPS[m - 1]), out)
        out = jnp.where(offset == minus, F32(-TAPS[m - 1]), out)
    return out


def kernel(
    shots, doms, fwd, adj, cn, cc, cs, buoy, wav, res, src, rcv, out,
    V, S, T, C, B, E, Q, RI, GL, GX, RL, RX, MZ, MY,
    load_sem, ssem, rsem, gs_sem, gr_sem,
):
    nx, ny, nz = B.shape
    rows = nx * ny
    yp = ny // shots
    dom = lax.axis_index("dom")
    shot = lax.axis_index("shot")
    has_lo = dom > 0
    has_hi = dom < doms - 1
    above = lax.rem(dom + 1, doms)
    below = lax.rem(dom + doms - 1, doms)

    loads = []

    def load(a, b):
        c = pltpu.make_async_copy(a, b, load_sem.at[len(loads)])
        c.start()
        loads.append(c)

    states = (fwd, adj)
    for w in range(2):
        load(states[w].at[0, 0:3], V.at[w, :, pl.ds(4, nx)])
    for w in range(2):
        load(states[w].at[0, 3], S.at[w, 0, pl.ds(4, nx)])
        load(states[w].at[0, 8], S.at[w, 1, pl.ds(4, nx)])
        load(states[w].at[0, 7], S.at[w, 2, pl.ds(4, nx)])
        load(states[w].at[0, 4:7], T.at[w])
    load(cn, C.at[0:3])
    load(cc, C.at[3:6])
    load(cs, C.at[6:9])
    load(buoy, B)

    barrier = pltpu.get_barrier_semaphore()

    @pl.when(has_lo)
    def _():
        pl.semaphore_signal(barrier, inc=1, device_id={"dom": below}, device_id_type=MESH)

    @pl.when(has_hi)
    def _():
        pl.semaphore_signal(barrier, inc=1, device_id={"dom": above}, device_id_type=MESH)

    for o in range(1, shots):
        pl.semaphore_signal(
            barrier, inc=1, device_id={"shot": lax.rem(shot + o, shots)}, device_id_type=MESH
        )

    @pl.when(jnp.logical_not(has_lo))
    def _():
        V[:, :, 0:4] = jnp.zeros((2, 3, 4, ny, nz), F32)
        S[:, :, 0:4] = jnp.zeros((2, 3, 4, ny, nz), F32)

    @pl.when(jnp.logical_not(has_hi))
    def _():
        V[:, :, 4 + nx : 8 + nx] = jnp.zeros((2, 3, 4, ny, nz), F32)
        S[:, :, 4 + nx : 8 + nx] = jnp.zeros((2, 3, 4, ny, nz), F32)

    pl.semaphore_wait(
        barrier, has_lo.astype(jnp.int32) + has_hi.astype(jnp.int32) + (shots - 1)
    )

    def message(stage, w, comp, side):
        buf = S if stage % 2 else V
        count = (VEL_LAYERS, STR_LAYERS)[stage % 2][side][comp]
        at, to = (4, 4 + nx) if side else (4 + nx - count, 4 - count)
        if stage == 0:
            source = states[w].at[0, comp, pl.ds(at - 4, count)]
        else:
            source = buf.at[w, comp, pl.ds(at, count)]
        return pltpu.make_async_remote_copy(
            src_ref=source,
            dst_ref=buf.at[w, comp, pl.ds(to, count)],
            send_sem=ssem.at[stage, w, side, comp],
            recv_sem=rsem.at[stage, w, side, comp],
            device_id={"dom": below if side else above},
            device_id_type=MESH,
        )

    def send(stage, w, comp):
        @pl.when(has_hi)
        def _():
            message(stage, w, comp, 0).start()

        @pl.when(has_lo)
        def _():
            message(stage, w, comp, 1).start()

    def wait_send(stage, w, comps):
        @pl.when(has_hi)
        def _():
            for comp in comps:
                message(stage, w, comp, 0).wait_send()

        @pl.when(has_lo)
        def _():
            for comp in comps:
                message(stage, w, comp, 1).wait_send()

    def wait_recv(stage, w, comp):
        @pl.when(has_lo)
        def _():
            message(stage, w, comp, 0).wait_recv()

        @pl.when(has_hi)
        def _():
            message(stage, w, comp, 1).wait_recv()

    for w in range(2):
        for comp in range(3):
            send(0, w, comp)

    r = lax.broadcasted_iota(jnp.int32, (nz, nz), 0)
    c = lax.broadcasted_iota(jnp.int32, (nz, nz), 1)
    for f in range(2):
        hi, mid = split2(band(r - c, f == 1))
        half = jnp.concatenate([hi, mid], axis=1)
        MZ[f] = jnp.concatenate([half, half], axis=0)
    r = lax.broadcasted_iota(jnp.int32, (rows, rows), 0)
    c = lax.broadcasted_iota(jnp.int32, (rows, rows), 1)
    for f in range(2):
        coef = jnp.where(r // ny == c // ny, band(c - r, f == 1), F32(0.0))
        hi, mid = split2(coef)
        half = jnp.concatenate([hi, mid], axis=0)
        MY[f] = jnp.concatenate([half, half], axis=1)

    cell = rcv[...]
    local = cell - dom * (rows * nz)
    cell_row = local // nz
    cell_z = local - nz * cell_row
    nrec = cell.shape[1]
    at_row = lax.broadcasted_iota(jnp.int32, (rows, nrec), 0) == cell_row
    at_z = (lax.broadcasted_iota(jnp.int32, (nz, nrec), 0) == cell_z).astype(F32).astype(BF16)
    for k in range(ITERS - 1):
        a = jnp.where(at_row, res[k], F32(0.0))
        hi, mid = split2(a)
        low = (a - hi.astype(F32) - mid.astype(F32)).astype(BF16)
        total = None
        for part in (low, mid, hi):
            d = lax.dot_general(
                part, at_z, (((1,), (1,)), ((), ())), preferred_element_type=F32
            )
            total = d if total is None else total + d
        RI[k] = total.reshape(nx, ny, nz)

    def zd(fields, forward):
        f = fields.reshape(-1, nz)
        hi, mid = split2(f)
        d = jnp.dot(
            jnp.concatenate([hi, mid], axis=1), MZ[int(forward)], preferred_element_type=F32
        )
        return (d[:, :nz] + d[:, nz:]).reshape(fields.shape)

    def yd(field, forward):
        hi, mid = split2(field.reshape(rows, nz))
        d = jnp.dot(
            MY[int(forward)], jnp.concatenate([hi, mid], axis=0), preferred_element_type=F32
        )
        return (d[:rows] + d[rows:]).reshape(nx, ny, nz)

    def xd(buf, w, comp, forward):
        total = None
        for m in range(1, 5):
            p, q = (m, 1 - m) if forward else (m - 1, -m)
            t = F32(TAPS[m - 1]) * (
                buf[w, comp, 4 + p : 4 + p + nx] - buf[w, comp, 4 + q : 4 + q + nx]
            )
            total = t if total is None else total + t
        return total

    def own(buf, w, comp):
        return buf[w, comp, 4 : 4 + nx]

    def local_strains(w):
        E[w, 1] = yd(own(V, w, 1), False)
        E[w, 2] = zd(own(V, w, 2), False)
        E[w, 3] = zd(own(V, w, 1), True) + yd(own(V, w, 2), True)
        E[w, 4] = zd(own(V, w, 0), True)
        E[w, 5] = yd(own(V, w, 0), True)

    def x_strain(w, comp):
        if comp == 0:
            E[w, 0] = xd(V, w, 0, False)
        else:
            at = 6 - comp
            E[w, at] = E[w, at] + xd(V, w, comp, True)

    def put(g, i, value, first):
        for p in range(shots):
            part = value[:, p * yp : (p + 1) * yp, :]
            g[p, i] = part if first else g[p, i] + part

    def image_local(first):
        put(GL, 0, E[0, 1] * E[1, 1], first)
        put(GL, 1, E[0, 2] * E[1, 2], first)
        put(GL, 2, E[0, 1] * E[1, 2] + E[0, 2] * E[1, 1], first)
        put(GL, 3, E[0, 3] * E[1, 3], first)
        put(
            GL, 4,
            own(V, 0, 0) * own(V, 1, 0) + own(V, 0, 1) * own(V, 1, 1)
            + own(V, 0, 2) * own(V, 1, 2),
            first,
        )

    def image_xx(first):
        put(GX, 0, E[0, 0] * E[1, 0], first)
        put(GX, 1, E[0, 0] * E[1, 1] + E[0, 1] * E[1, 0], first)
        put(GX, 2, E[0, 0] * E[1, 2] + E[0, 2] * E[1, 0], first)

    def image_shear(first):
        put(GX, 3, E[0, 4] * E[1, 4], first)
        put(GX, 4, E[0, 5] * E[1, 5], first)

    def source_field(k):
        at = (
            lax.broadcasted_iota(jnp.int32, (nx, ny, nz), 0) * (ny * nz)
            + lax.broadcasted_iota(jnp.int32, (nx, ny, nz), 1) * nz
            + lax.broadcasted_iota(jnp.int32, (nx, ny, nz), 2)
        )
        return jnp.where(at == src[0] - dom * (rows * nz), wav[0, k], F32(0.0))

    def signed(w, base, change):
        return base + change if w else base - change

    groups = ((GL, RL, 0, 5), (GX, RX, 0, 3), (GX, RX, 3, 2))

    def sums(group):
        g, landing, at, count = groups[group]
        copies = []
        for o in range(1, shots):
            to = lax.rem(shot + o, shots)
            copies.append(
                pltpu.make_async_remote_copy(
                    src_ref=g.at[to, pl.ds(at, count)],
                    dst_ref=landing.at[o - 1, pl.ds(at, count)],
                    send_sem=gs_sem.at[group, o - 1],
                    recv_sem=gr_sem.at[group, o - 1],
                    device_id={"shot": to},
                    device_id_type=MESH,
                )
            )
        return copies

    loads[0].wait()
    loads[1].wait()
    for k in range(ITERS):
        for w in range(2):
            local_strains(w)
        if k == ITERS - 1:
            break
        if k == 0:
            for copy in loads[2:]:
                copy.wait()
        for w in range(2):
            for comp in range(3):
                wait_recv(2 * k, w, comp)
                x_strain(w, comp)
                if k:
                    wait_send(2 * k - 1, w, (comp,))
                if comp == 0:
                    change = C[0] * E[w, 0] + C[3] * E[w, 1] + C[4] * E[w, 2]
                else:
                    change = C[9 - comp] * E[w, 6 - comp]
                stress = signed(w, own(S, w, comp), change)
                if w == 0 and comp == 0:
                    stress = stress - source_field(k)
                S[w, comp, 4 : 4 + nx] = stress
                send(2 * k + 1, w, comp)
        for w in range(2):
            exx, eyy, ezz = E[w, 0], E[w, 1], E[w, 2]
            syy = signed(w, T[w, 0], C[3] * exx + C[1] * eyy + C[5] * ezz)
            szz = signed(w, T[w, 1], C[4] * exx + C[5] * eyy + C[2] * ezz)
            if w == 0:
                pulse = source_field(k)
                syy = syy - pulse
                szz = szz - pulse
            syz = signed(w, T[w, 2], C[6] * E[w, 3])
            T[w, 0] = syy
            T[w, 1] = szz
            T[w, 2] = syz
            Q[w, 0] = yd(own(S, w, 1), False) + zd(own(S, w, 2), False)
            Q[w, 1] = yd(syy, True) + zd(syz, False)
            Q[w, 2] = yd(syz, False) + zd(szz, True)
        image_local(k == 0)
        image_xx(k == 0)
        image_shear(k == 0)
        for w in range(2):
            for comp in range(3):
                wait_recv(2 * k + 1, w, comp)
                change = B[...] * (xd(S, w, comp, comp == 0) + Q[w, comp])
                velocity = signed(w, own(V, w, comp), change)
                if w == 1 and comp == 2:
                    velocity = velocity + RI[k]
                if k:
                    wait_send(2 * k, w, (comp,))
                V[w, comp, 4 : 4 + nx] = velocity
                send(2 * k + 2, w, comp)

    image_local(False)
    for copy in sums(0):
        copy.start()
    for comp in range(3):
        for w in range(2):
            wait_recv(2 * ITERS - 2, w, comp)
            x_strain(w, comp)
        if comp == 0:
            image_xx(False)
            for copy in sums(1):
                copy.start()
    image_shear(False)
    for copy in sums(2):
        copy.start()
    slots = ((1, 2, 5, 6, 9), (0, 3, 4), (7, 8))
    for group, (g, landing, at, count) in enumerate(groups):
        for copy in sums(group):
            copy.wait_recv()
        for i, slot in enumerate(slots[group]):
            total = g[shot, at + i]
            for o in range(shots - 1):
                total = total + landing[o, at + i]
            out[slot] = total
    for w in range(2):
        for stage in (0, 2 * ITERS - 3, 2 * ITERS - 2):
            wait_send(stage, w, range(3))
    for group in range(3):
        for copy in sums(group):
            copy.wait_send()


def body(shots, doms, fwd, adj, cn, cc, cs, buoy, wav, res, src, rcv):
    nx, ny, nz = buoy.shape
    field = (nx, ny, nz)
    yp = ny // shots
    wide = nx + 8
    stages = 2 * ITERS - 1
    hbm = pl.BlockSpec(memory_space=pltpu.HBM)
    vmem = pl.BlockSpec(memory_space=pltpu.VMEM)
    smem = pl.BlockSpec(memory_space=pltpu.SMEM)
    summed = pl.pallas_call(
        functools.partial(kernel, shots, doms),
        out_shape=jax.ShapeDtypeStruct((10, nx, yp, nz), F32),
        in_specs=[hbm] * 6 + [smem, vmem, smem, vmem],
        out_specs=vmem,
        scratch_shapes=[
            pltpu.VMEM((2, 3, wide, ny, nz), F32),
            pltpu.VMEM((2, 3, wide, ny, nz), F32),
            pltpu.VMEM((2, 3) + field, F32),
            pltpu.VMEM((9,) + field, F32),
            pltpu.VMEM(field, F32),
            pltpu.VMEM((2, 6) + field, F32),
            pltpu.VMEM((2, 3) + field, F32),
            pltpu.VMEM((ITERS - 1,) + field, F32),
            pltpu.VMEM((shots, 5, nx, yp, nz), F32),
            pltpu.VMEM((shots, 5, nx, yp, nz), F32),
            pltpu.VMEM((shots - 1, 5, nx, yp, nz), F32),
            pltpu.VMEM((shots - 1, 5, nx, yp, nz), F32),
            pltpu.VMEM((2, 2 * nz, 2 * nz), BF16),
            pltpu.VMEM((2, 2 * nx * ny, 2 * nx * ny), BF16),
            pltpu.SemaphoreType.DMA((14,)),
            pltpu.SemaphoreType.DMA((stages, 2, 2, 3)),
            pltpu.SemaphoreType.DMA((stages, 2, 2, 3)),
            pltpu.SemaphoreType.DMA((3, shots - 1)),
            pltpu.SemaphoreType.DMA((3, shots - 1)),
        ],
        compiler_params=pltpu.CompilerParams(
            collective_id=0, has_side_effects=True, vmem_limit_bytes=63 * 1024 * 1024
        ),
    )(fwd, adj, cn, cc, cs, buoy, wav, jnp.transpose(res, (1, 0, 2)), src, rcv)
    return summed / ITERS


def solution(mesh):
    placed = (
        P("shot", None, "dom", None, None),
        P("shot", None, "dom", None, None),
        P(None, "dom", None, None),
        P(None, "dom", None, None),
        P(None, "dom", None, None),
        P("dom", None, None),
        P("shot", None),
        P("shot", None, None),
        P("shot"),
        P("shot", None),
    )
    return jax.shard_map(
        functools.partial(body, mesh.shape["shot"], mesh.shape["dom"]),
        mesh=mesh,
        in_specs=placed,
        out_specs=P(None, "dom", "shot", None),
        check_vma=False,
    )
```
